32 devices in a mesh: groups: 2 (over y), cube: 4 (over z), row: 2 (over x), pair: 2 (over core).
Axes of the slice: x: 2, y: 2, z: 4, core: 2. Of those that a mesh axis runs over, the one named last changes fastest.
Arguments:
- ligand: float32 [2, 64, 32, 1024], P('pair', ('groups', 'cube', 'row')), parts along dimension 1, may hold values from 0.05 to 3
- density: int32 [64, 32, 1024], P(('groups', 'cube', 'row')), parts along dimension 0, may hold values from 0 to 7
- counts: int32 [16], P(('groups', 'cube', 'row')), parts along dimension 0, may hold values from 1 to 4, as said below
- neighbours: int32 [64, 6], P(('groups', 'cube', 'row')), parts along dimension 0, may hold values from -1 to 31, as said below
- diffusion: float32 [2], replicated, may hold values from 0.04 to 0.14
- uptake: float32 [2], replicated, may hold values from 0.03 to 0.18
Outputs:
- ligand_out: float32 [2, 64, 32, 1024], P('pair', ('groups', 'cube', 'row')), parts along dimension 1
The draws below stay inside these ranges and needn't reach their ends.
There are 2 independent parts, one for each index of `groups`. The reference program is written for one: setup_inputs(seed, part) draws one part's arguments, and reference() takes and returns one part's arrays. A program takes and returns all parts, laid end to end along the dimension named above; an argument that names none is the same for every part. Nothing has to cross between parts.
Inputs may be any that keep to these rules, and one draw needn't show every extreme that they name: `counts`: the number of occupied tiles of each block of 4 slots; they fill the first slots of their block; some block is full and some block holds 1. Block b = layer * 2 + band holds tile slots b * 4 to (b + 1) * 4 - 1; an entry is -1 for an empty slot, for a face on the volume's boundary and for an unoccupied place; x neighbours lie in the same block, a -y neighbour in block b or b - 1, a +y neighbour in block b or b + 1, a -z neighbour in block b - 2, a +z neighbour in block b + 2; if tile u names v across a face, v names u across the opposite face.
All inputs are finite; a program needn't handle non-finite values.
Results may differ from the reference program's by a relative error of at most 0.00007.
Values sent between devices are 32-bit elements; how exact they have to be, the bound alone decides.
A program may use at most 64 MiB of HBM per device.

```python
import math
import jax
import jax.numpy as jnp

EX = 32
EY = 32
EZ = 32
TXN = 12
TYB = 3
SLOTS = 4
STEPS = 4
LAYERS = 4
BANDS = 2
TILES = 32


def shuffle_places(key):
    return jax.random.permutation(key, TXN * TYB)


def tissue_layout(key):
    blocks = LAYERS * BANDS
    key = jax.random.fold_in(key, 4711)
    k_count, k_full, k_thin, k_perm = jax.random.split(key, 4)
    occupied = jax.random.randint(k_count, (blocks,), SLOTS // 4, SLOTS + 1)
    full_block = jax.random.randint(k_full, (), 0, blocks)
    thin_block = (full_block + 1 + jax.random.randint(k_thin, (), 0, blocks - 1)) % blocks
    order = jnp.arange(blocks, dtype=jnp.int32)
    occupied = jnp.where(order == full_block, SLOTS, jnp.where(order == thin_block, SLOTS // 4, occupied))
    layouts = jax.vmap(shuffle_places)(jax.random.split(k_perm, blocks)).astype(jnp.int32)
    rank = jnp.argsort(layouts, axis=1).astype(jnp.int32)
    slot_at = jnp.where(rank < occupied[:, None], rank, -1)
    place = layouts[:, :SLOTS]
    column_x = place // TYB
    column_y = place % TYB
    blk = jnp.broadcast_to(order[:, None], place.shape)
    layer = blk // BANDS
    band = blk % BANDS

    def locate(target_block, target_place, allowed):
        safe_block = jnp.clip(target_block, 0, blocks - 1)
        safe_place = jnp.clip(target_place, 0, TXN * TYB - 1)
        found = slot_at[safe_block, safe_place]
        good = allowed & (found >= 0)
        return jnp.where(good, safe_block * SLOTS + found, -1)
    minus_x = locate(blk, place - TYB, column_x > 0)
    plus_x = locate(blk, place + TYB, column_x < TXN - 1)
    inside_low = column_y > 0
    minus_y = locate(jnp.where(inside_low, blk, blk - 1), jnp.where(inside_low, place - 1, place + TYB - 1), inside_low | (band > 0))
    inside_high = column_y < TYB - 1
    plus_y = locate(jnp.where(inside_high, blk, blk + 1), jnp.where(inside_high, place + 1, place - (TYB - 1)), inside_high | (band < BANDS - 1))
    minus_z = locate(blk - BANDS, place, layer > 0)
    plus_z = locate(blk + BANDS, place, layer < LAYERS - 1)
    table = jnp.stack([minus_x, plus_x, minus_y, plus_y, minus_z, plus_z], -1)
    live = jnp.arange(SLOTS, dtype=jnp.int32)[None, :] < occupied[:, None]
    table = jnp.where(live[:, :, None], table, -1).reshape(blocks * SLOTS, 6)
    return (occupied.astype(jnp.int32), table.astype(jnp.int32))


def draw_counts(key, part):
    return tissue_layout(key)[0]


def draw_neighbours(key, part):
    return tissue_layout(key)[1]


def set_ends(result, rng, low, high):
    longest = result.shape.index(max(result.shape))
    spots = []
    for shift in (0, 1):
        where = [jax.random.randint(jax.random.fold_in(rng, axis), (), 0, length) for axis, length in enumerate(result.shape)]
        where[longest] = (where[longest] + shift) % result.shape[longest]
        spots.append(tuple(where))
    return result.at[spots[0]].set(low).at[spots[1]].set(high)


def block_levels(key, extent, cuts, low, top_value):
    gain = 1.0
    for axis_at, blocks in cuts:
        heights = jax.random.uniform(jax.random.fold_in(jax.random.fold_in(key, 6), axis_at), (blocks,), jnp.float32, low / len(cuts), top_value / len(cuts))
        gain = gain * jnp.repeat(jnp.exp(heights), extent[axis_at] // blocks).reshape((-1,) + (1,) * (len(extent) - 1 - axis_at))
    return gain


def setup_inputs(seed: int = 0, part: int = 0) -> dict:
    arg_keys = jax.random.split(jax.random.key(seed), 7)
    own_keys = jax.random.split(jax.random.fold_in(arg_keys[6], part), 7)
    return {
        "ligand": jnp.clip(jnp.exp(math.log(3.0) - 4.0943445 * jax.random.uniform(own_keys[0], (2, TILES, EZ, EX * EY), jnp.float32) ** block_levels(own_keys[0], (2, TILES, EZ, EX * EY), ((0, 2), (1, 8)), -0.2, 0.2)), 0.05, 3.0),
        "density": set_ends(jax.random.randint(own_keys[1], (TILES, EZ, EX * EY), 0, 8), jax.random.fold_in(own_keys[1], 1), 0, 7).astype(jnp.int32),
        "counts": draw_counts(jax.random.fold_in(jax.random.fold_in(arg_keys[6], part), 71), part),
        "neighbours": draw_neighbours(jax.random.fold_in(jax.random.fold_in(arg_keys[6], part), 71), part),
        "diffusion": jnp.clip(jax.random.uniform(arg_keys[4], (2,), jnp.float32, 0.04, 0.14), 0.04, 0.14),
        "uptake": jnp.clip(jnp.exp(jax.random.uniform(arg_keys[5], (2,), jnp.float32, math.log(0.03), math.log(0.18))), 0.03, 0.18),
    }


def ghost_cells(face, column, neighbours):
    index = neighbours[:, column]
    picked = jnp.take(face, jnp.clip(index, 0, TILES - 1), axis=1)
    okay = (index >= 0).reshape((1, -1, 1, 1, 1))
    return jnp.where(okay, picked, jnp.float32(0.0))


def neighbour_sum(field, neighbours):
    x_minus = jnp.concatenate([ghost_cells(field[:, :, :, -1:, :], 0, neighbours), field[:, :, :, :-1, :]], 3)
    x_plus = jnp.concatenate([field[:, :, :, 1:, :], ghost_cells(field[:, :, :, :1, :], 1, neighbours)], 3)
    y_minus = jnp.concatenate([ghost_cells(field[:, :, :, :, -1:], 2, neighbours), field[:, :, :, :, :-1]], 4)
    y_plus = jnp.concatenate([field[:, :, :, :, 1:], ghost_cells(field[:, :, :, :, :1], 3, neighbours)], 4)
    z_minus = jnp.concatenate([ghost_cells(field[:, :, -1:], 4, neighbours), field[:, :, :-1]], 2)
    z_plus = jnp.concatenate([field[:, :, 1:], ghost_cells(field[:, :, :1], 5, neighbours)], 2)
    return x_minus + x_plus + y_minus + y_plus + z_minus + z_plus


def reference(ligand, density, counts, neighbours, diffusion, uptake):
    field = ligand.reshape(2, TILES, EZ, EX, EY)
    scaled = density.reshape(TILES, EZ, EX, EY).astype(jnp.float32) / 8.0
    slot_ids = jnp.arange(TILES, dtype=jnp.int32) % SLOTS
    filled = slot_ids < jnp.repeat(counts, SLOTS)
    field = jnp.where(filled.reshape(1, -1, 1, 1, 1), field, jnp.float32(0.0))
    rate = diffusion.reshape(2, 1, 1, 1, 1)
    rate_up = uptake.reshape(2, 1, 1, 1, 1)
    for step in range(STEPS):
        total = field[0] + field[1]
        nsum = neighbour_sum(field, neighbours)
        field = field + rate * (nsum - 6.0 * field) - rate_up * scaled[None] * field / (1.0 + total)[None]
    return field.reshape(2, TILES, EZ, EX * EY)
```

```python
import functools

import jax
import jax.numpy as jnp
from jax import lax
from jax.experimental import pallas as pl
from jax.experimental.pallas import tpu as pltpu
from jax.sharding import PartitionSpec as P

EY = 32
STEPS = 4
LANES = 128
ROWS = 8
MESH = pl.DeviceIdType.MESH


def kernel(
    layers, bands, slots, half, cells,
    nbr, counts, diffusion, uptake, ligand, density, out,
    field, dens, stage, y_own, y_minus, y_plus, z_low, z_high, z_minus, z_plus,
    load_sem, swap_send, swap_recv, face_send, face_recv, out_send, out_recv,
):
    core = lax.axis_index("pair")
    layer = lax.axis_index("cube")
    band = lax.axis_index("row")
    block = layer * bands + band
    other = 1 - core
    columns = cells // LANES
    has_minus = band > 0
    has_plus = band < bands - 1
    far_layer = jnp.where(core == 0, layer - 1, layer + 1)
    has_far = jnp.logical_and(far_layer >= 0, far_layer < layers)
    partner_id = {"pair": other}
    far_id = {"cube": far_layer, "pair": other}
    minus_id = {"row": band - 1}
    plus_id = {"row": band + 1}

    own_rows = pl.ds(pl.multiple_of(core * half, half), half)
    other_rows = pl.ds(pl.multiple_of(other * half, half), half)
    loads = [
        pltpu.make_async_copy(ligand.at[0, :, own_rows, :], field.at[0, core], load_sem.at[0]),
        pltpu.make_async_copy(density.at[:, own_rows, :], dens, load_sem.at[1]),
    ]
    for load in loads:
        load.start()

    barrier = pltpu.get_barrier_semaphore()
    pl.semaphore_signal(barrier, inc=1, device_id=partner_id, device_id_type=MESH)

    @pl.when(has_far)
    def _():
        pl.semaphore_signal(barrier, inc=1, device_id=far_id, device_id_type=MESH)

    @pl.when(has_minus)
    def _():
        pl.semaphore_signal(barrier, inc=1, device_id=minus_id, device_id_type=MESH)

    @pl.when(has_plus)
    def _():
        pl.semaphore_signal(barrier, inc=1, device_id=plus_id, device_id_type=MESH)

    peers = 1 + has_far.astype(jnp.int32) + has_minus.astype(jnp.int32) + has_plus.astype(jnp.int32)
    pl.semaphore_wait(barrier, peers)

    swap = pltpu.make_async_remote_copy(
        src_ref=ligand.at[0, :, other_rows, :], dst_ref=field.at[0, core],
        send_sem=swap_send, recv_sem=swap_recv, device_id=partner_id, device_id_type=MESH,
    )
    swap_in = pltpu.make_async_remote_copy(
        src_ref=ligand.at[0, :, other_rows, :], dst_ref=field.at[0, other],
        send_sem=swap_send, recv_sem=swap_recv, device_id=partner_id, device_id_type=MESH,
    )
    swap.start()

    def remote(source, target, step, k, device):
        return pltpu.make_async_remote_copy(
            src_ref=source.at[step], dst_ref=target[step],
            send_sem=face_send.at[step, k], recv_sem=face_recv.at[step, k],
            device_id=device, device_id_type=MESH,
        )

    def messages(step):
        first, last = core == 0, core == 1
        up_far = remote(z_high, z_minus, step, 0, far_id)
        up_near = remote(z_high, z_minus, step, 0, partner_id)
        down_far = remote(z_low, z_plus, step, 1, far_id)
        down_near = remote(z_low, z_plus, step, 1, partner_id)
        to_plus = remote(y_own, y_minus, step, 2, plus_id)
        to_minus = remote(y_own, y_plus, step, 3, minus_id)
        both = jnp.logical_and
        sends = [
            (both(last, has_far), up_far), (first, up_near),
            (both(first, has_far), down_far), (last, down_near),
            (has_plus, to_plus), (has_minus, to_minus),
        ]
        receives = [
            (jnp.logical_or(last, has_far), up_near), (jnp.logical_or(first, has_far), down_near),
            (has_minus, to_plus), (has_plus, to_minus),
        ]
        return sends, receives

    def send_faces(step):
        for wanted, copy in messages(step)[0]:
            pl.when(wanted)(copy.start)

    def wait_faces(step):
        for wanted, copy in messages(step)[1]:
            pl.when(wanted)(copy.wait_recv)

    def wait_sent(step):
        for wanted, copy in messages(step)[0]:
            pl.when(wanted)(copy.wait_send)

    lane = lax.broadcasted_iota(jnp.int32, (ROWS, LANES), 1)
    pair_of = lax.rem(lane + 1, EY) // 2
    even = lax.rem(lane, 2) == 0
    wide = lax.broadcasted_iota(jnp.int32, (half, LANES), 1)
    at_low = lax.rem(wide, EY) == 0
    at_high = lax.rem(wide, EY) == EY - 1
    below_32 = wide < EY
    above_96 = wide >= LANES - EY

    def roll(value, shift):
        shift = shift % LANES
        return value if shift == 0 else pltpu.roll(value, shift, axis=1)

    pieces = [(zv, j) for zv in range(half // ROWS) for j in range(columns)]

    def put_faces(step, species, tile, parts):
        packed = None
        for m, (zv, j) in enumerate(pieces):
            piece = roll(parts[j][zv * ROWS : (zv + 1) * ROWS], 2 * m)
            packed = piece if packed is None else jnp.where(pair_of == m, piece, packed)
        y_own[step, species, tile] = packed
        for j in range(columns):
            at = slice(j * LANES, (j + 1) * LANES)
            z_low[step, species, tile, :, at] = parts[j][:1]
            z_high[step, species, tile, :, at] = parts[j][half - 1 :]

    def columns_of(value):
        return [value[:, j * LANES : (j + 1) * LANES] for j in range(columns)]

    def first_faces(tile, carry):
        for species in range(2):
            put_faces(0, species, tile, columns_of(field[0, species, tile]))
        return carry

    zero = jnp.float32(0.0)

    def advance(step, tile):
        now, later = step % 2, (step + 1) % 2
        filled = tile < counts[0]

        def entry(k):
            value = nbr[tile, k]
            safe = jnp.maximum(value, 0)
            return value >= 0, lax.rem(safe, slots), safe // slots == block

        left_ok, left, _ = entry(0)
        right_ok, right, _ = entry(1)
        front_ok, front, front_here = entry(2)
        back_ok, back, back_here = entry(3)
        lower_ok, lower, _ = entry(4)
        upper_ok, upper, _ = entry(5)
        first = core == 0
        lower = jnp.where(first, lower, tile)
        lower_ok = jnp.where(first, lower_ok, filled)
        upper = jnp.where(first, tile, upper)
        upper_ok = jnp.where(first, filled, upper_ok)

        fields, sums = [], []
        for species in range(2):
            parts = columns_of(field[now, species, tile])
            if step == 0:
                parts = [jnp.where(filled, part, zero) for part in parts]
            ghost_left = roll(field[now, species, left, :, cells - LANES :], EY)
            ghost_right = roll(field[now, species, right, :, :LANES], -EY)
            forward = [jnp.where(left_ok, ghost_left, zero)] + [roll(part, EY) for part in parts]
            backward = [roll(part, -EY) for part in parts] + [jnp.where(right_ok, ghost_right, zero)]
            from_front = jnp.where(
                front_here, y_own[step, species, front], y_minus[step][species, front]
            )
            from_back = jnp.where(back_here, y_own[step, species, back], y_plus[step][species, back])
            from_front = jnp.where(front_ok, from_front, zero)
            from_back = jnp.where(back_ok, from_back, zero)
            ghost_y = jnp.where(even, roll(from_front, 1 - EY), roll(from_back, EY - 1))
            below = jnp.where(lower_ok, z_minus[step][species, lower], zero)
            above = jnp.where(upper_ok, z_plus[step][species, upper], zero)
            total = []
            for j in range(columns):
                part = parts[j]
                at = slice(j * LANES, (j + 1) * LANES)
                edge = jnp.concatenate(
                    [
                        roll(ghost_y, -2 * (zv * columns + j))
                        for zv in range(half // ROWS)
                    ],
                    axis=0,
                )
                value = jnp.where(below_32, forward[j], forward[j + 1])
                value = value + jnp.where(above_96, backward[j + 1], backward[j])
                value = value + jnp.where(at_low, edge, roll(part, 1))
                value = value + jnp.where(at_high, edge, roll(part, -1))
                value = value + jnp.concatenate([below[:, at], part[: half - 1]], axis=0)
                value = value + jnp.concatenate([part[1:], above[:, at]], axis=0)
                total.append(value)
            fields.append(parts)
            sums.append(total)
        amount = columns_of(dens[tile])
        share = [
            amount[j].astype(jnp.float32) / (1.0 + fields[0][j] + fields[1][j])
            for j in range(columns)
        ]
        result = []
        for species in range(2):
            rate = diffusion[species]
            keep = 1.0 - 6.0 * rate
            taken = uptake[species] * 0.125
            result.append(
                [
                    fields[species][j] * (keep - taken * share[j]) + rate * sums[species][j]
                    for j in range(columns)
                ]
            )
        return later, result

    def one_step(step):
        def body(tile, carry):
            later, result = advance(step, tile)
            for species in range(2):
                for j in range(columns):
                    at = slice(j * LANES, (j + 1) * LANES)
                    field[later, species, tile, :, at] = result[species][j]
                put_faces(step + 1, species, tile, result[species])
            return carry

        lax.fori_loop(0, slots, body, 0)

    def give(tile):
        return pltpu.make_async_remote_copy(
            src_ref=stage.at[tile], dst_ref=out.at[0, tile, own_rows, :],
            send_sem=out_send.at[tile], recv_sem=out_recv.at[tile],
            device_id=partner_id, device_id_type=MESH,
        )

    def take(tile):
        return pltpu.make_async_remote_copy(
            src_ref=stage.at[tile], dst_ref=out.at[0, tile, other_rows, :],
            send_sem=out_send.at[tile], recv_sem=out_recv.at[tile],
            device_id=partner_id, device_id_type=MESH,
        )

    for load in loads:
        load.wait()
    swap_in.wait_recv()
    lax.fori_loop(0, slots, first_faces, 0)
    send_faces(0)
    for step in range(STEPS - 1):
        wait_faces(step)
        one_step(step)
        send_faces(step + 1)
    wait_faces(STEPS - 1)

    def last_body(tile, carry):
        _, result = advance(STEPS - 1, tile)
        for j in range(columns):
            at = slice(j * LANES, (j + 1) * LANES)
            stage[tile, :, at] = jnp.where(core == 0, result[1][j], result[0][j])
        give(tile).start()
        for j in range(columns):
            at = slice(j * LANES, (j + 1) * LANES)
            out[0, tile, own_rows, at] = jnp.where(core == 0, result[0][j], result[1][j])
        return carry

    lax.fori_loop(0, slots, last_body, 0)
    swap.wait_send()
    for step in range(STEPS):
        wait_sent(step)
    for tile in range(slots):
        give(tile).wait_send()
        take(tile).wait_recv()


def per_device(layers, bands, ligand, density, counts, neighbours, diffusion, uptake):
    _, slots, depth, cells = ligand.shape
    half = depth // 2
    faces = (2, slots, ROWS, LANES)
    planes = (2, slots, 1, cells)
    smem = pl.BlockSpec(memory_space=pltpu.SMEM)
    away = pl.BlockSpec(memory_space=pl.ANY)
    return pl.pallas_call(
        functools.partial(kernel, layers, bands, slots, half, cells),
        out_shape=jax.ShapeDtypeStruct(ligand.shape, jnp.float32),
        in_specs=[smem, smem, smem, smem, away, away],
        out_specs=pl.BlockSpec(memory_space=pltpu.VMEM),
        scratch_shapes=[
            pltpu.VMEM((2, 2, slots, half, cells), jnp.float32),
            pltpu.VMEM((slots, half, cells), jnp.int32),
            pltpu.VMEM((slots, half, cells), jnp.float32),
            pltpu.VMEM((STEPS,) + faces, jnp.float32),
            [pltpu.VMEM(faces, jnp.float32)] * STEPS,
            [pltpu.VMEM(faces, jnp.float32)] * STEPS,
            pltpu.VMEM((STEPS,) + planes, jnp.float32),
            pltpu.VMEM((STEPS,) + planes, jnp.float32),
            [pltpu.VMEM(planes, jnp.float32)] * STEPS,
            [pltpu.VMEM(planes, jnp.float32)] * STEPS,
            pltpu.SemaphoreType.DMA((2,)),
            pltpu.SemaphoreType.DMA,
            pltpu.SemaphoreType.DMA,
            pltpu.SemaphoreType.DMA((STEPS, 4)),
            pltpu.SemaphoreType.DMA((STEPS, 4)),
            pltpu.SemaphoreType.DMA((slots,)),
            pltpu.SemaphoreType.DMA((slots,)),
        ],
        compiler_params=pltpu.CompilerParams(
            collective_id=0, has_side_effects=True, vmem_limit_bytes=32 * 1024 * 1024
        ),
    )(neighbours, counts, diffusion, uptake, ligand, density)


def solution(mesh):
    in_specs = (
        P("pair", ("groups", "cube", "row"), None, None),
        P(("groups", "cube", "row"), None, None),
        P(("groups", "cube", "row")),
        P(("groups", "cube", "row"), None),
        P(),
        P(),
    )
    out_specs = P("pair", ("groups", "cube", "row"), None, None)
    return jax.shard_map(
        functools.partial(per_device, mesh.shape["cube"], mesh.shape["row"]),
        mesh=mesh, in_specs=in_specs, out_specs=out_specs, check_vma=False,
    )
```

```python
import functools

import jax
import jax.numpy as jnp
from jax import lax
from jax.experimental import pallas as pl
from jax.experimental.pallas import tpu as pltpu
from jax.sharding import PartitionSpec as P

EY = 32
STEPS = 4
LANES = 128
ROWS = 8
MESH = pl.DeviceIdType.MESH


def kernel(
    layers, bands, slots, half, cells,
    nbr, counts, diffusion, uptake, ligand, density, out,
    field, dens, stage, y_high, y_low, y_minus, y_plus, z_low, z_high, z_minus, z_plus,
    load_sem, swap_send, swap_recv, face_send, face_recv, out_send, out_recv,
):
    core = lax.axis_index("pair")
    layer = lax.axis_index("cube")
    band = lax.axis_index("row")
    block = layer * bands + band
    other = 1 - core
    columns = cells // LANES
    has_minus = band > 0
    has_plus = band < bands - 1
    far_layer = jnp.where(core == 0, layer - 1, layer + 1)
    has_far = jnp.logical_and(far_layer >= 0, far_layer < layers)
    partner_id = {"pair": other}
    far_id = {"cube": far_layer, "pair": other}
    minus_id = {"row": band - 1}
    plus_id = {"row": band + 1}

    own_rows = pl.ds(pl.multiple_of(core * half, half), half)
    other_rows = pl.ds(pl.multiple_of(other * half, half), half)
    loads = [
        pltpu.make_async_copy(ligand.at[0, :, own_rows, :], field.at[0, core], load_sem.at[0]),
        pltpu.make_async_copy(density.at[:, own_rows, :], dens, load_sem.at[1]),
    ]
    for load in loads:
        load.start()

    barrier = pltpu.get_barrier_semaphore()
    pl.semaphore_signal(barrier, inc=1, device_id=partner_id, device_id_type=MESH)

    @pl.when(has_far)
    def _():
        pl.semaphore_signal(barrier, inc=1, device_id=far_id, device_id_type=MESH)

    @pl.when(has_minus)
    def _():
        pl.semaphore_signal(barrier, inc=1, device_id=minus_id, device_id_type=MESH)

    @pl.when(has_plus)
    def _():
        pl.semaphore_signal(barrier, inc=1, device_id=plus_id, device_id_type=MESH)

    peers = 1 + has_far.astype(jnp.int32) + has_minus.astype(jnp.int32) + has_plus.astype(jnp.int32)
    pl.semaphore_wait(barrier, peers)

    swap = pltpu.make_async_remote_copy(
        src_ref=ligand.at[0, :, other_rows, :], dst_ref=field.at[0, core],
        send_sem=swap_send, recv_sem=swap_recv, device_id=partner_id, device_id_type=MESH,
    )
    swap_in = pltpu.make_async_remote_copy(
        src_ref=ligand.at[0, :, other_rows, :], dst_ref=field.at[0, other],
        send_sem=swap_send, recv_sem=swap_recv, device_id=partner_id, device_id_type=MESH,
    )
    swap.start()

    def remote(source, target, step, k, device):
        return pltpu.make_async_remote_copy(
            src_ref=source.at[step], dst_ref=target[step],
            send_sem=face_send.at[step, k], recv_sem=face_recv.at[step, k],
            device_id=device, device_id_type=MESH,
        )

    def messages(step):
        first, last = core == 0, core == 1
        up_far = remote(z_high, z_minus, step, 0, far_id)
        up_near = remote(z_high, z_minus, step, 0, partner_id)
        down_far = remote(z_low, z_plus, step, 1, far_id)
        down_near = remote(z_low, z_plus, step, 1, partner_id)
        to_plus = remote(y_high, y_minus, step, 2, plus_id)
        to_minus = remote(y_low, y_plus, step, 3, minus_id)
        both = jnp.logical_and
        sends = [
            (both(last, has_far), up_far), (first, up_near),
            (both(first, has_far), down_far), (last, down_near),
            (has_plus, to_plus), (has_minus, to_minus),
        ]
        receives = [
            (jnp.logical_or(last, has_far), up_near), (jnp.logical_or(first, has_far), down_near),
            (has_minus, to_plus), (has_plus, to_minus),
        ]
        return sends, receives

    def send_faces(step):
        for wanted, copy in messages(step)[0]:
            pl.when(wanted)(copy.start)

    def wait_faces(step):
        for wanted, copy in messages(step)[1]:
            pl.when(wanted)(copy.wait_recv)

    def wait_sent(step):
        for wanted, copy in messages(step)[0]:
            pl.when(wanted)(copy.wait_send)

    lane = lax.broadcasted_iota(jnp.int32, (ROWS, LANES), 1)
    pair_of = lax.rem(lane + 1, EY) // 2
    even = lax.rem(lane, 2) == 0
    wide = lax.broadcasted_iota(jnp.int32, (half, LANES), 1)
    at_low = lax.rem(wide, EY) == 0
    at_high = lax.rem(wide, EY) == EY - 1
    at_edge = jnp.logical_or(at_low, at_high)
    below_32 = wide < EY
    above_96 = wide >= LANES - EY

    def roll(value, shift):
        shift = shift % LANES
        return value if shift == 0 else pltpu.roll(value, shift, axis=1)

    pieces = [(zv, j) for zv in range(half // ROWS) for j in range(columns)]

    def put_faces(step, tile, both):
        packed = []
        for species in range(2):
            parts = both[species]
            total = None
            for m, (zv, j) in enumerate(pieces):
                piece = roll(parts[j][zv * ROWS : (zv + 1) * ROWS], 2 * m)
                total = piece if total is None else jnp.where(pair_of == m, piece, total)
            packed.append(total)
            for j in range(columns):
                at = slice(j * LANES, (j + 1) * LANES)
                z_low[step, species, tile, :, at] = parts[j][:1]
                z_high[step, species, tile, :, at] = parts[j][half - 1 :]
        second = roll(packed[1], 1)
        y_low[step, tile] = jnp.where(even, packed[0], second)
        y_high[step, tile] = jnp.where(even, second, packed[0])

    def columns_of(value):
        return [value[:, j * LANES : (j + 1) * LANES] for j in range(columns)]

    def first_faces(tile, carry):
        put_faces(0, tile, [columns_of(field[0, species, tile]) for species in range(2)])
        return carry

    zero = jnp.float32(0.0)
    row = lax.broadcasted_iota(jnp.int32, (half, LANES), 0)

    def entry(tile, k):
        value = nbr[tile, k]
        safe = jnp.maximum(value, 0)
        return value >= 0, lax.rem(safe, slots), safe // slots == block

    def inner(step, tile):
        now, later = step % 2, (step + 1) % 2
        filled = tile < counts[0]
        left_ok, left, _ = entry(tile, 0)
        right_ok, right, _ = entry(tile, 1)
        fields = []
        for species in range(2):
            parts = columns_of(field[now, species, tile])
            if step == 0:
                parts = [jnp.where(filled, part, zero) for part in parts]
            fields.append(parts)
        amount = columns_of(dens[tile])
        share = [
            amount[j].astype(jnp.float32) / (1.0 + fields[0][j] + fields[1][j])
            for j in range(columns)
        ]
        blank = jnp.zeros((1, LANES), jnp.float32)
        for species in range(2):
            parts = fields[species]
            rate = diffusion[species]
            keep = 1.0 - 6.0 * rate
            taken = uptake[species] * 0.125
            ghost_left = roll(field[now, species, left, :, cells - LANES :], EY)
            ghost_right = roll(field[now, species, right, :, :LANES], -EY)
            forward = [jnp.where(left_ok, ghost_left, zero)] + [roll(part, EY) for part in parts]
            backward = [roll(part, -EY) for part in parts] + [jnp.where(right_ok, ghost_right, zero)]
            for j in range(columns):
                part = parts[j]
                value = jnp.where(below_32, forward[j], forward[j + 1])
                value = value + jnp.where(above_96, backward[j + 1], backward[j])
                value = value + jnp.where(at_low, zero, roll(part, 1))
                value = value + jnp.where(at_high, zero, roll(part, -1))
                value = value + jnp.concatenate([blank, part[: half - 1]], axis=0)
                value = value + jnp.concatenate([part[1:], blank], axis=0)
                at = slice(j * LANES, (j + 1) * LANES)
                field[later, species, tile, :, at] = (
                    part * (keep - taken * share[j]) + rate * value
                )

    def outer(step, tile):
        later = (step + 1) % 2
        filled = tile < counts[0]
        front_ok, front, front_here = entry(tile, 2)
        back_ok, back, back_here = entry(tile, 3)
        lower_ok, lower, _ = entry(tile, 4)
        upper_ok, upper, _ = entry(tile, 5)
        first = core == 0
        lower = jnp.where(first, lower, tile)
        lower_ok = jnp.where(first, lower_ok, filled)
        upper = jnp.where(first, tile, upper)
        upper_ok = jnp.where(first, filled, upper_ok)
        from_front = jnp.where(front_here, y_high[step, front], y_minus[step][front])
        from_back = jnp.where(back_here, y_low[step, back], y_plus[step][back])
        from_front = jnp.where(front_ok, from_front, zero)
        from_back = jnp.where(back_ok, from_back, zero)
        result = []
        for species in range(2):
            rate = diffusion[species]
            ghost_y = rate * jnp.where(
                even, roll(from_front, 1 - EY - species), roll(from_back, EY - 1 - species)
            )
            below = rate * jnp.where(lower_ok, z_minus[step][species, lower], zero)
            above = rate * jnp.where(upper_ok, z_plus[step][species, upper], zero)
            values = []
            for j in range(columns):
                at = slice(j * LANES, (j + 1) * LANES)
                edge = jnp.concatenate(
                    [roll(ghost_y, -2 * (zv * columns + j)) for zv in range(half // ROWS)], axis=0
                )
                value = field[later, species, tile, :, at] + jnp.where(at_edge, edge, zero)
                value = value + jnp.where(row == 0, below[:, at], zero)
                value = value + jnp.where(row == half - 1, above[:, at], zero)
                values.append(value)
            result.append(values)
        return result

    def inner_step(step):
        def body(tile, carry):
            inner(step, tile)
            return carry

        lax.fori_loop(0, slots, body, 0, unroll=True)

    def outer_step(step):
        later = (step + 1) % 2

        def body(tile, carry):
            result = outer(step, tile)
            for species in range(2):
                for j in range(columns):
                    at = slice(j * LANES, (j + 1) * LANES)
                    field[later, species, tile, :, at] = result[species][j]
            put_faces(step + 1, tile, result)
            return carry

        lax.fori_loop(0, slots, body, 0, unroll=True)

    def give(tile):
        return pltpu.make_async_remote_copy(
            src_ref=stage.at[tile], dst_ref=out.at[0, tile, own_rows, :],
            send_sem=out_send.at[tile], recv_sem=out_recv.at[tile],
            device_id=partner_id, device_id_type=MESH,
        )

    def take(tile):
        return pltpu.make_async_remote_copy(
            src_ref=stage.at[tile], dst_ref=out.at[0, tile, other_rows, :],
            send_sem=out_send.at[tile], recv_sem=out_recv.at[tile],
            device_id=partner_id, device_id_type=MESH,
        )

    for load in loads:
        load.wait()
    swap_in.wait_recv()
    lax.fori_loop(0, slots, first_faces, 0)
    send_faces(0)
    for step in range(STEPS - 1):
        inner_step(step)
        wait_faces(step)
        outer_step(step)
        send_faces(step + 1)
    inner_step(STEPS - 1)
    wait_faces(STEPS - 1)

    def last_body(tile, carry):
        result = outer(STEPS - 1, tile)
        for j in range(columns):
            at = slice(j * LANES, (j + 1) * LANES)
            stage[tile, :, at] = jnp.where(core == 0, result[1][j], result[0][j])
        give(tile).start()
        for j in range(columns):
            at = slice(j * LANES, (j + 1) * LANES)
            out[0, tile, own_rows, at] = jnp.where(core == 0, result[0][j], result[1][j])
        return carry

    lax.fori_loop(0, slots, last_body, 0)
    swap.wait_send()
    for step in range(STEPS):
        wait_sent(step)
    for tile in range(slots):
        give(tile).wait_send()
        take(tile).wait_recv()


def per_device(layers, bands, ligand, density, counts, neighbours, diffusion, uptake):
    _, slots, depth, cells = ligand.shape
    half = depth // 2
    faces = (slots, ROWS, LANES)
    planes = (2, slots, 1, cells)
    smem = pl.BlockSpec(memory_space=pltpu.SMEM)
    away = pl.BlockSpec(memory_space=pltpu.HBM)
    return pl.pallas_call(
        functools.partial(kernel, layers, bands, slots, half, cells),
        out_shape=jax.ShapeDtypeStruct(ligand.shape, jnp.float32),
        in_specs=[smem, smem, smem, smem, away, away],
        out_specs=pl.BlockSpec(memory_space=pltpu.VMEM),
        scratch_shapes=[
            pltpu.VMEM((2, 2, slots, half, cells), jnp.float32),
            pltpu.VMEM((slots, half, cells), jnp.int32),
            pltpu.VMEM((slots, half, cells), jnp.float32),
            pltpu.VMEM((STEPS,) + faces, jnp.float32),
            pltpu.VMEM((STEPS,) + faces, jnp.float32),
            [pltpu.VMEM(faces, jnp.float32)] * STEPS,
            [pltpu.VMEM(faces, jnp.float32)] * STEPS,
            pltpu.VMEM((STEPS,) + planes, jnp.float32),
            pltpu.VMEM((STEPS,) + planes, jnp.float32),
            [pltpu.VMEM(planes, jnp.float32)] * STEPS,
            [pltpu.VMEM(planes, jnp.float32)] * STEPS,
            pltpu.SemaphoreType.DMA((2,)),
            pltpu.SemaphoreType.DMA,
            pltpu.SemaphoreType.DMA,
            pltpu.SemaphoreType.DMA((STEPS, 4)),
            pltpu.SemaphoreType.DMA((STEPS, 4)),
            pltpu.SemaphoreType.DMA((slots,)),
            pltpu.SemaphoreType.DMA((slots,)),
        ],
        compiler_params=pltpu.CompilerParams(
            collective_id=0, has_side_effects=True, vmem_limit_bytes=56 * 1024 * 1024
        ),
    )(neighbours, counts, diffusion, uptake, ligand, density)


def solution(mesh):
    in_specs = (
        P("pair", ("groups", "cube", "row"), None, None),
        P(("groups", "cube", "row"), None, None),
        P(("groups", "cube", "row")),
        P(("groups", "cube", "row"), None),
        P(),
        P(),
    )
    out_specs = P("pair", ("groups", "cube", "row"), None, None)
    return jax.shard_map(
        functools.partial(per_device, mesh.shape["cube"], mesh.shape["row"]),
        mesh=mesh, in_specs=in_specs, out_specs=out_specs, check_vma=False,
    )
```

```python
import functools

import jax
import jax.numpy as jnp
from jax import lax
from jax.experimental import pallas as pl
from jax.experimental.pallas import tpu as pltpu
from jax.sharding import PartitionSpec as P

EY = 32
STEPS = 4
LANES = 128
ROWS = 8
MESH = pl.DeviceIdType.MESH


def kernel(
    layers, bands, slots, half, cells,
    nbr, counts, diffusion, uptake, ligand, density, out,
    field, dens, stage, y_high, y_low, y_minus, y_plus, z_low, z_high, z_minus, z_plus,
    extra, y_first, y_here, z_first_low, z_first_high, first_send, first_recv,
    load_sem, swap_send, swap_recv, face_send, face_recv, out_send, out_recv,
):
    core = lax.axis_index("pair")
    layer = lax.axis_index("cube")
    band = lax.axis_index("row")
    block = layer * bands + band
    other = 1 - core
    columns = cells // LANES
    has_minus = band > 0
    has_plus = band < bands - 1
    far_layer = jnp.where(core == 0, layer - 1, layer + 1)
    has_far = jnp.logical_and(far_layer >= 0, far_layer < layers)
    partner_id = {"pair": other}
    far_id = {"cube": far_layer, "pair": other}
    minus_id = {"row": band - 1}
    plus_id = {"row": band + 1}

    own_rows = pl.ds(pl.multiple_of(core * half, half), half)
    other_rows = pl.ds(pl.multiple_of(other * half, half), half)
    loads = [
        pltpu.make_async_copy(ligand.at[0, :, own_rows, :], field.at[0, core], load_sem.at[0]),
        pltpu.make_async_copy(ligand.at[0, :, other_rows, :], extra, load_sem.at[2]),
        pltpu.make_async_copy(density.at[:, own_rows, :], dens, load_sem.at[1]),
    ]
    for load in loads:
        load.start()

    barrier = pltpu.get_barrier_semaphore()
    has_down = layer > 0
    has_up = layer < layers - 1
    always = layer >= 0
    greeted = [
        (always, partner_id),
        (has_far, far_id),
        (has_down, {"cube": layer - 1}),
        (has_up, {"cube": layer + 1}),
        (has_minus, minus_id),
        (has_plus, plus_id),
        (has_minus, {"row": band - 1, "pair": other}),
        (has_plus, {"row": band + 1, "pair": other}),
    ]
    peers = jnp.int32(0)
    for wanted, device in greeted:
        pl.when(wanted)(
            functools.partial(
                pl.semaphore_signal, barrier, inc=1, device_id=device, device_id_type=MESH
            )
        )
        peers = peers + wanted.astype(jnp.int32)
    pl.semaphore_wait(barrier, peers)

    swap = pltpu.make_async_remote_copy(
        src_ref=ligand.at[0, :, other_rows, :], dst_ref=field.at[0, core],
        send_sem=swap_send, recv_sem=swap_recv, device_id=partner_id, device_id_type=MESH,
    )
    swap_in = pltpu.make_async_remote_copy(
        src_ref=ligand.at[0, :, other_rows, :], dst_ref=field.at[0, other],
        send_sem=swap_send, recv_sem=swap_recv, device_id=partner_id, device_id_type=MESH,
    )
    swap.start()

    def remote(source, target, step, k, device):
        return pltpu.make_async_remote_copy(
            src_ref=source.at[step], dst_ref=target[step],
            send_sem=face_send.at[step, k], recv_sem=face_recv.at[step, k],
            device_id=device, device_id_type=MESH,
        )

    def messages(step):
        first, last = core == 0, core == 1
        up_far = remote(z_high, z_minus, step, 0, far_id)
        up_near = remote(z_high, z_minus, step, 0, partner_id)
        down_far = remote(z_low, z_plus, step, 1, far_id)
        down_near = remote(z_low, z_plus, step, 1, partner_id)
        to_plus = remote(y_high, y_minus, step, 2, plus_id)
        to_minus = remote(y_low, y_plus, step, 3, minus_id)
        both = jnp.logical_and
        sends = [
            (both(last, has_far), up_far), (first, up_near),
            (both(first, has_far), down_far), (last, down_near),
            (has_plus, to_plus), (has_minus, to_minus),
        ]
        receives = [
            (jnp.logical_or(last, has_far), up_near), (jnp.logical_or(first, has_far), down_near),
            (has_minus, to_plus), (has_plus, to_minus),
        ]
        return sends, receives

    def first_copy(source, target, k, at, device):
        return pltpu.make_async_remote_copy(
            src_ref=source, dst_ref=target.at[core],
            send_sem=first_send.at[k], recv_sem=first_recv.at[at, core],
            device_id=device, device_id_type=MESH,
        )

    def first_sends():
        return [
            (core == 0, first_copy(z_first_high.at[0], z_minus[0], 0, 0, partner_id)),
            (core == 1, first_copy(z_first_low.at[1], z_plus[0], 1, 1, partner_id)),
            (has_down, first_copy(
                z_first_low.at[0], z_plus[0], 2, 1, {"cube": layer - 1, "pair": core * 0 + 1})),
            (has_up, first_copy(
                z_first_high.at[1], z_minus[0], 3, 0, {"cube": layer + 1, "pair": core * 0})),
        ] + [
            (has_plus, first_copy(
                y_first.at[h], y_minus[0], 4 + h, 2, {"row": band + 1, "pair": core * 0 + h}))
            for h in range(2)
        ] + [
            (has_minus, first_copy(
                y_first.at[h], y_plus[0], 6 + h, 3, {"row": band - 1, "pair": core * 0 + h}))
            for h in range(2)
        ]

    def arrived(target, at, species):
        pltpu.make_async_remote_copy(
            src_ref=target.at[species], dst_ref=target.at[species],
            send_sem=first_send.at[0], recv_sem=first_recv.at[at, species],
            device_id=partner_id, device_id_type=MESH,
        ).wait_recv()

    def wait_first():
        both, either = jnp.logical_and, jnp.logical_or
        for species in range(2):
            across = core == 1 - species
            minus = either(both(core == 0, has_down), both(core == 1, across))
            plus = either(both(core == 1, has_up), both(core == 0, across))
            pl.when(minus)(functools.partial(arrived, z_minus[0], 0, species))
            pl.when(plus)(functools.partial(arrived, z_plus[0], 1, species))
            pl.when(has_minus)(functools.partial(arrived, y_minus[0], 2, species))
            pl.when(has_plus)(functools.partial(arrived, y_plus[0], 3, species))

    def send_faces(step):
        for wanted, copy in messages(step)[0]:
            pl.when(wanted)(copy.start)

    def wait_faces(step):
        for wanted, copy in messages(step)[1]:
            pl.when(wanted)(copy.wait_recv)

    def wait_sent(step):
        for wanted, copy in messages(step)[0]:
            pl.when(wanted)(copy.wait_send)

    lane = lax.broadcasted_iota(jnp.int32, (ROWS, LANES), 1)
    pair_of = lax.rem(lane + 1, EY) // 2
    even = lax.rem(lane, 2) == 0
    wide = lax.broadcasted_iota(jnp.int32, (half, LANES), 1)
    at_low = lax.rem(wide, EY) == 0
    at_high = lax.rem(wide, EY) == EY - 1
    at_edge = jnp.logical_or(at_low, at_high)
    below_32 = wide < EY
    above_96 = wide >= LANES - EY

    def roll(value, shift):
        shift = shift % LANES
        return value if shift == 0 else pltpu.roll(value, shift, axis=1)

    pieces = [(zv, j) for zv in range(half // ROWS) for j in range(columns)]

    def pack(parts):
        total = None
        for m, (zv, j) in enumerate(pieces):
            piece = roll(parts[j][zv * ROWS : (zv + 1) * ROWS], 2 * m)
            total = piece if total is None else jnp.where(pair_of == m, piece, total)
        return total

    def put_faces(step, tile, both):
        packed = []
        for species in range(2):
            parts = both[species]
            packed.append(pack(parts))
            for j in range(columns):
                at = slice(j * LANES, (j + 1) * LANES)
                z_low[step, species, tile, :, at] = parts[j][:1]
                z_high[step, species, tile, :, at] = parts[j][half - 1 :]
        second = roll(packed[1], 1)
        y_low[step, tile] = jnp.where(even, packed[0], second)
        y_high[step, tile] = jnp.where(even, second, packed[0])

    def columns_of(value):
        return [value[:, j * LANES : (j + 1) * LANES] for j in range(columns)]

    def first_faces(tile, carry):
        for h, value in ((core, field[0, core, tile]), (other, extra[tile])):
            packed = pack(columns_of(value))
            y_first[h, tile] = packed
            z_first_low[h, tile] = value[:1]
            z_first_high[h, tile] = value[half - 1 :]
            if h is core:
                y_here[core, tile] = packed
        return carry

    def other_faces(tile, carry):
        y_here[other, tile] = pack(columns_of(field[0, other, tile]))
        return carry

    def own_planes():
        @pl.when(core == 0)
        def _():
            z_plus[0][0] = z_first_low[1]

        @pl.when(core == 1)
        def _():
            z_minus[0][1] = z_first_high[0]

    zero = jnp.float32(0.0)
    row = lax.broadcasted_iota(jnp.int32, (half, LANES), 0)

    def entry(tile, k):
        value = nbr[tile, k]
        safe = jnp.maximum(value, 0)
        return value >= 0, lax.rem(safe, slots), safe // slots == block

    def inner(step, tile):
        now, later = step % 2, (step + 1) % 2
        filled = tile < counts[0]
        left_ok, left, _ = entry(tile, 0)
        right_ok, right, _ = entry(tile, 1)
        fields = []
        for species in range(2):
            parts = columns_of(field[now, species, tile])
            if step == 0:
                parts = [jnp.where(filled, part, zero) for part in parts]
            fields.append(parts)
        amount = columns_of(dens[tile])
        share = [
            amount[j].astype(jnp.float32) / (1.0 + fields[0][j] + fields[1][j])
            for j in range(columns)
        ]
        blank = jnp.zeros((1, LANES), jnp.float32)
        for species in range(2):
            parts = fields[species]
            rate = diffusion[species]
            keep = 1.0 - 6.0 * rate
            taken = uptake[species] * 0.125
            ghost_left = roll(field[now, species, left, :, cells - LANES :], EY)
            ghost_right = roll(field[now, species, right, :, :LANES], -EY)
            forward = [jnp.where(left_ok, ghost_left, zero)] + [roll(part, EY) for part in parts]
            backward = [roll(part, -EY) for part in parts] + [jnp.where(right_ok, ghost_right, zero)]
            for j in range(columns):
                part = parts[j]
                value = jnp.where(below_32, forward[j], forward[j + 1])
                value = value + jnp.where(above_96, backward[j + 1], backward[j])
                value = value + jnp.where(at_low, zero, roll(part, 1))
                value = value + jnp.where(at_high, zero, roll(part, -1))
                value = value + jnp.concatenate([blank, part[: half - 1]], axis=0)
                value = value + jnp.concatenate([part[1:], blank], axis=0)
                at = slice(j * LANES, (j + 1) * LANES)
                field[later, species, tile, :, at] = (
                    part * (keep - taken * share[j]) + rate * value
                )

    def outer(step, tile):
        later = (step + 1) % 2
        filled = tile < counts[0]
        front_ok, front, front_here = entry(tile, 2)
        back_ok, back, back_here = entry(tile, 3)
        lower_ok, lower, _ = entry(tile, 4)
        upper_ok, upper, _ = entry(tile, 5)
        first = core == 0
        lower = jnp.where(first, lower, tile)
        lower_ok = jnp.where(first, lower_ok, filled)
        upper = jnp.where(first, tile, upper)
        upper_ok = jnp.where(first, filled, upper_ok)
        result = []
        for species in range(2):
            rate = diffusion[species]
            if step == 0:
                shift = 0
                from_front = jnp.where(front_here, y_here[species, front], y_minus[0][species, front])
                from_back = jnp.where(back_here, y_here[species, back], y_plus[0][species, back])
            else:
                shift = species
                from_front = jnp.where(front_here, y_high[step, front], y_minus[step][front])
                from_back = jnp.where(back_here, y_low[step, back], y_plus[step][back])
            from_front = jnp.where(front_ok, from_front, zero)
            from_back = jnp.where(back_ok, from_back, zero)
            ghost_y = rate * jnp.where(
                even, roll(from_front, 1 - EY - shift), roll(from_back, EY - 1 - shift)
            )
            below = rate * jnp.where(lower_ok, z_minus[step][species, lower], zero)
            above = rate * jnp.where(upper_ok, z_plus[step][species, upper], zero)
            values = []
            for j in range(columns):
                at = slice(j * LANES, (j + 1) * LANES)
                edge = jnp.concatenate(
                    [roll(ghost_y, -2 * (zv * columns + j)) for zv in range(half // ROWS)], axis=0
                )
                value = field[later, species, tile, :, at] + jnp.where(at_edge, edge, zero)
                value = value + jnp.where(row == 0, below[:, at], zero)
                value = value + jnp.where(row == half - 1, above[:, at], zero)
                values.append(value)
            result.append(values)
        return result

    def inner_step(step):
        def body(tile, carry):
            inner(step, tile)
            return carry

        lax.fori_loop(0, slots, body, 0, unroll=True)

    def outer_step(step):
        later = (step + 1) % 2

        def body(tile, carry):
            result = outer(step, tile)
            for species in range(2):
                for j in range(columns):
                    at = slice(j * LANES, (j + 1) * LANES)
                    field[later, species, tile, :, at] = result[species][j]
            put_faces(step + 1, tile, result)
            return carry

        lax.fori_loop(0, slots, body, 0, unroll=True)

    def give(tile):
        return pltpu.make_async_remote_copy(
            src_ref=stage.at[tile], dst_ref=out.at[0, tile, own_rows, :],
            send_sem=out_send.at[tile], recv_sem=out_recv.at[tile],
            device_id=partner_id, device_id_type=MESH,
        )

    def take(tile):
        return pltpu.make_async_remote_copy(
            src_ref=stage.at[tile], dst_ref=out.at[0, tile, other_rows, :],
            send_sem=out_send.at[tile], recv_sem=out_recv.at[tile],
            device_id=partner_id, device_id_type=MESH,
        )

    loads[0].wait()
    loads[1].wait()
    lax.fori_loop(0, slots, first_faces, 0, unroll=True)
    for wanted, copy in first_sends():
        pl.when(wanted)(copy.start)
    own_planes()
    loads[2].wait()
    swap_in.wait_recv()
    lax.fori_loop(0, slots, other_faces, 0, unroll=True)
    for step in range(STEPS):
        inner_step(step)
        if step == 0:
            wait_first()
        else:
            wait_faces(step)
        if step < STEPS - 1:
            outer_step(step)
            send_faces(step + 1)

    def last_body(tile, carry):
        result = outer(STEPS - 1, tile)
        for j in range(columns):
            at = slice(j * LANES, (j + 1) * LANES)
            stage[tile, :, at] = jnp.where(core == 0, result[1][j], result[0][j])
        give(tile).start()
        for j in range(columns):
            at = slice(j * LANES, (j + 1) * LANES)
            out[0, tile, own_rows, at] = jnp.where(core == 0, result[0][j], result[1][j])
        return carry

    lax.fori_loop(0, slots, last_body, 0)
    swap.wait_send()
    for wanted, copy in first_sends():
        pl.when(wanted)(copy.wait_send)
    for step in range(1, STEPS):
        wait_sent(step)
    for tile in range(slots):
        give(tile).wait_send()
        take(tile).wait_recv()


def per_device(layers, bands, ligand, density, counts, neighbours, diffusion, uptake):
    _, slots, depth, cells = ligand.shape
    half = depth // 2
    faces = (slots, ROWS, LANES)
    planes = (2, slots, 1, cells)
    smem = pl.BlockSpec(memory_space=pltpu.SMEM)
    away = pl.BlockSpec(memory_space=pltpu.HBM)
    return pl.pallas_call(
        functools.partial(kernel, layers, bands, slots, half, cells),
        out_shape=jax.ShapeDtypeStruct(ligand.shape, jnp.float32),
        in_specs=[smem, smem, smem, smem, away, away],
        out_specs=pl.BlockSpec(memory_space=pltpu.VMEM),
        scratch_shapes=[
            pltpu.VMEM((2, 2, slots, half, cells), jnp.float32),
            pltpu.VMEM((slots, half, cells), jnp.int32),
            pltpu.VMEM((slots, half, cells), jnp.float32),
            pltpu.VMEM((STEPS,) + faces, jnp.float32),
            pltpu.VMEM((STEPS,) + faces, jnp.float32),
            [pltpu.VMEM((2,) + faces, jnp.float32)] + [pltpu.VMEM(faces, jnp.float32)] * (STEPS - 1),
            [pltpu.VMEM((2,) + faces, jnp.float32)] + [pltpu.VMEM(faces, jnp.float32)] * (STEPS - 1),
            pltpu.VMEM((STEPS,) + planes, jnp.float32),
            pltpu.VMEM((STEPS,) + planes, jnp.float32),
            [pltpu.VMEM(planes, jnp.float32)] * STEPS,
            [pltpu.VMEM(planes, jnp.float32)] * STEPS,
            pltpu.VMEM((slots, half, cells), jnp.float32),
            pltpu.VMEM((2,) + faces, jnp.float32),
            pltpu.VMEM((2,) + faces, jnp.float32),
            pltpu.VMEM(planes, jnp.float32),
            pltpu.VMEM(planes, jnp.float32),
            pltpu.SemaphoreType.DMA((8,)),
            pltpu.SemaphoreType.DMA((4, 2)),
            pltpu.SemaphoreType.DMA((3,)),
            pltpu.SemaphoreType.DMA,
            pltpu.SemaphoreType.DMA,
            pltpu.SemaphoreType.DMA((STEPS, 4)),
            pltpu.SemaphoreType.DMA((STEPS, 4)),
            pltpu.SemaphoreType.DMA((slots,)),
            pltpu.SemaphoreType.DMA((slots,)),
        ],
        compiler_params=pltpu.CompilerParams(
            collective_id=0, has_side_effects=True, vmem_limit_bytes=53 * 1024 * 1024
        ),
    )(neighbours, counts, diffusion, uptake, ligand, density)


def solution(mesh):
    in_specs = (
        P("pair", ("groups", "cube", "row"), None, None),
        P(("groups", "cube", "row"), None, None),
        P(("groups", "cube", "row")),
        P(("groups", "cube", "row"), None),
        P(),
        P(),
    )
    out_specs = P("pair", ("groups", "cube", "row"), None, None)
    return jax.shard_map(
        functools.partial(per_device, mesh.shape["cube"], mesh.shape["row"]),
        mesh=mesh, in_specs=in_specs, out_specs=out_specs, check_vma=False,
    )
```

```python
import functools

import jax
import jax.numpy as jnp
from jax import lax
from jax.experimental import pallas as pl
from jax.experimental.pallas import tpu as pltpu
from jax.sharding import PartitionSpec as P

EY = 32
STEPS = 4
LANES = 128
ROWS = 8
MESH = pl.DeviceIdType.MESH


def kernel(
    layers, bands, slots, half, cells,
    nbr, counts, diffusion, uptake, ligand, density, out,
    field, dens, stage, y_high, y_low, y_minus, y_plus, z_low, z_high, z_minus, z_plus,
    extra, y_first, y_here, z_first_low, z_first_high, first_send, first_recv,
    load_sem, swap_send, swap_recv, face_send, face_recv, out_send, out_recv,
):
    core = lax.axis_index("pair")
    layer = lax.axis_index("cube")
    band = lax.axis_index("row")
    block = layer * bands + band
    other = 1 - core
    columns = cells // LANES
    has_minus = band > 0
    has_plus = band < bands - 1
    far_layer = jnp.where(core == 0, layer - 1, layer + 1)
    has_far = jnp.logical_and(far_layer >= 0, far_layer < layers)
    partner_id = {"pair": other}
    far_id = {"cube": far_layer, "pair": other}
    minus_id = {"row": band - 1}
    plus_id = {"row": band + 1}

    own_rows = pl.ds(pl.multiple_of(core * half, half), half)
    other_rows = pl.ds(pl.multiple_of(other * half, half), half)
    loads = [
        pltpu.make_async_copy(ligand.at[0, :, own_rows, :], field.at[0, core], load_sem.at[0]),
        pltpu.make_async_copy(ligand.at[0, :, other_rows, :], extra, load_sem.at[2]),
        pltpu.make_async_copy(density.at[:, own_rows, :], dens, load_sem.at[1]),
    ]
    for load in loads:
        load.start()

    barrier = pltpu.get_barrier_semaphore()
    has_down = layer > 0
    has_up = layer < layers - 1
    always = layer >= 0
    greeted = [
        (always, partner_id),
        (has_far, far_id),
        (has_down, {"cube": layer - 1}),
        (has_up, {"cube": layer + 1}),
        (has_minus, minus_id),
        (has_plus, plus_id),
        (has_minus, {"row": band - 1, "pair": other}),
        (has_plus, {"row": band + 1, "pair": other}),
    ]
    peers = jnp.int32(0)
    for wanted, device in greeted:
        pl.when(wanted)(
            functools.partial(
                pl.semaphore_signal, barrier, inc=1, device_id=device, device_id_type=MESH
            )
        )
        peers = peers + wanted.astype(jnp.int32)
    pl.semaphore_wait(barrier, peers)

    swap = pltpu.make_async_remote_copy(
        src_ref=ligand.at[0, :, other_rows, :], dst_ref=field.at[0, core],
        send_sem=swap_send, recv_sem=swap_recv, device_id=partner_id, device_id_type=MESH,
    )
    swap_in = pltpu.make_async_remote_copy(
        src_ref=ligand.at[0, :, other_rows, :], dst_ref=field.at[0, other],
        send_sem=swap_send, recv_sem=swap_recv, device_id=partner_id, device_id_type=MESH,
    )
    swap.start()

    def remote(source, target, step, k, device):
        return pltpu.make_async_remote_copy(
            src_ref=source.at[step], dst_ref=target[step],
            send_sem=face_send.at[step, k], recv_sem=face_recv.at[step, k],
            device_id=device, device_id_type=MESH,
        )

    def messages(step):
        first, last = core == 0, core == 1
        up_far = remote(z_high, z_minus, step, 0, far_id)
        up_near = remote(z_high, z_minus, step, 0, partner_id)
        down_far = remote(z_low, z_plus, step, 1, far_id)
        down_near = remote(z_low, z_plus, step, 1, partner_id)
        to_plus = remote(y_high, y_minus, step, 2, plus_id)
        to_minus = remote(y_low, y_plus, step, 3, minus_id)
        both = jnp.logical_and
        sends = [
            (has_plus, to_plus), (has_minus, to_minus),
            (both(last, has_far), up_far), (both(first, has_far), down_far),
            (first, up_near), (last, down_near),
        ]
        receives = [
            (jnp.logical_or(last, has_far), up_near), (jnp.logical_or(first, has_far), down_near),
            (has_minus, to_plus), (has_plus, to_minus),
        ]
        return sends, receives

    def first_copy(source, target, k, at, device):
        return pltpu.make_async_remote_copy(
            src_ref=source, dst_ref=target.at[core],
            send_sem=first_send.at[k], recv_sem=first_recv.at[at, core],
            device_id=device, device_id_type=MESH,
        )

    def first_sends():
        return [
            (core == 0, first_copy(z_first_high.at[0], z_minus[0], 0, 0, partner_id)),
            (core == 1, first_copy(z_first_low.at[1], z_plus[0], 1, 1, partner_id)),
            (has_down, first_copy(
                z_first_low.at[0], z_plus[0], 2, 1, {"cube": layer - 1, "pair": core * 0 + 1})),
            (has_up, first_copy(
                z_first_high.at[1], z_minus[0], 3, 0, {"cube": layer + 1, "pair": core * 0})),
        ] + [
            (has_plus, first_copy(
                y_first.at[h], y_minus[0], 4 + h, 2, {"row": band + 1, "pair": core * 0 + h}))
            for h in range(2)
        ] + [
            (has_minus, first_copy(
                y_first.at[h], y_plus[0], 6 + h, 3, {"row": band - 1, "pair": core * 0 + h}))
            for h in range(2)
        ]

    def arrived(target, at, species):
        pltpu.make_async_remote_copy(
            src_ref=target.at[species], dst_ref=target.at[species],
            send_sem=first_send.at[0], recv_sem=first_recv.at[at, species],
            device_id=partner_id, device_id_type=MESH,
        ).wait_recv()

    def wait_first():
        both, either = jnp.logical_and, jnp.logical_or
        for species in range(2):
            across = core == 1 - species
            minus = either(both(core == 0, has_down), both(core == 1, across))
            plus = either(both(core == 1, has_up), both(core == 0, across))
            pl.when(minus)(functools.partial(arrived, z_minus[0], 0, species))
            pl.when(plus)(functools.partial(arrived, z_plus[0], 1, species))
            pl.when(has_minus)(functools.partial(arrived, y_minus[0], 2, species))
            pl.when(has_plus)(functools.partial(arrived, y_plus[0], 3, species))

    def send_faces(step):
        for wanted, copy in messages(step)[0]:
            pl.when(wanted)(copy.start)

    def wait_faces(step):
        for wanted, copy in messages(step)[1]:
            pl.when(wanted)(copy.wait_recv)

    def wait_sent(step):
        for wanted, copy in messages(step)[0]:
            pl.when(wanted)(copy.wait_send)

    lane = lax.broadcasted_iota(jnp.int32, (ROWS, LANES), 1)
    pair_of = lax.rem(lane + 1, EY) // 2
    even = lax.rem(lane, 2) == 0
    wide = lax.broadcasted_iota(jnp.int32, (half, LANES), 1)
    at_low = lax.rem(wide, EY) == 0
    at_high = lax.rem(wide, EY) == EY - 1
    at_edge = jnp.logical_or(at_low, at_high)
    below_32 = wide < EY
    above_96 = wide >= LANES - EY

    def roll(value, shift):
        shift = shift % LANES
        return value if shift == 0 else pltpu.roll(value, shift, axis=1)

    pieces = [(zv, j) for zv in range(half // ROWS) for j in range(columns)]

    def pack(parts):
        total = None
        for m, (zv, j) in enumerate(pieces):
            piece = roll(parts[j][zv * ROWS : (zv + 1) * ROWS], 2 * m)
            total = piece if total is None else jnp.where(pair_of == m, piece, total)
        return total

    def put_faces(step, tile, both):
        packed = []
        for species in range(2):
            parts = both[species]
            packed.append(pack(parts))
            for j in range(columns):
                at = slice(j * LANES, (j + 1) * LANES)
                z_low[step, species, tile, :, at] = parts[j][:1]
                z_high[step, species, tile, :, at] = parts[j][half - 1 :]
        second = roll(packed[1], 1)
        y_low[step, tile] = jnp.where(even, packed[0], second)
        y_high[step, tile] = jnp.where(even, second, packed[0])

    def columns_of(value):
        return [value[:, j * LANES : (j + 1) * LANES] for j in range(columns)]

    def first_faces(tile, carry):
        for h, value in ((core, field[0, core, tile]), (other, extra[tile])):
            packed = pack(columns_of(value))
            y_first[h, tile] = packed
            z_first_low[h, tile] = value[:1]
            z_first_high[h, tile] = value[half - 1 :]
            if h is core:
                y_here[core, tile] = packed
        return carry

    def other_faces(tile, carry):
        y_here[other, tile] = pack(columns_of(field[0, other, tile]))
        return carry

    def own_planes():
        @pl.when(core == 0)
        def _():
            z_plus[0][0] = z_first_low[1]

        @pl.when(core == 1)
        def _():
            z_minus[0][1] = z_first_high[0]

    zero = jnp.float32(0.0)
    row = lax.broadcasted_iota(jnp.int32, (half, LANES), 0)

    def entry(tile, k):
        value = nbr[tile, k]
        safe = jnp.maximum(value, 0)
        return value >= 0, lax.rem(safe, slots), safe // slots == block

    def inner(step, tile):
        now, later = step % 2, (step + 1) % 2
        filled = tile < counts[0]
        left_ok, left, _ = entry(tile, 0)
        right_ok, right, _ = entry(tile, 1)
        fields = []
        for species in range(2):
            parts = columns_of(field[now, species, tile])
            if step == 0:
                parts = [jnp.where(filled, part, zero) for part in parts]
            fields.append(parts)
        amount = columns_of(dens[tile])
        share = [
            amount[j].astype(jnp.float32) / (1.0 + fields[0][j] + fields[1][j])
            for j in range(columns)
        ]
        blank = jnp.zeros((1, LANES), jnp.float32)
        for species in range(2):
            parts = fields[species]
            rate = diffusion[species]
            keep = 1.0 - 6.0 * rate
            taken = uptake[species] * 0.125
            ghost_left = roll(field[now, species, left, :, cells - LANES :], EY)
            ghost_right = roll(field[now, species, right, :, :LANES], -EY)
            forward = [jnp.where(left_ok, ghost_left, zero)] + [roll(part, EY) for part in parts]
            backward = [roll(part, -EY) for part in parts] + [jnp.where(right_ok, ghost_right, zero)]
            for j in range(columns):
                part = parts[j]
                value = jnp.where(below_32, forward[j], forward[j + 1])
                value = value + jnp.where(above_96, backward[j + 1], backward[j])
                value = value + jnp.where(at_low, zero, roll(part, 1))
                value = value + jnp.where(at_high, zero, roll(part, -1))
                value = value + jnp.concatenate([blank, part[: half - 1]], axis=0)
                value = value + jnp.concatenate([part[1:], blank], axis=0)
                at = slice(j * LANES, (j + 1) * LANES)
                field[later, species, tile, :, at] = (
                    part * (keep - taken * share[j]) + rate * value
                )

    def outer(step, tile):
        later = (step + 1) % 2
        filled = tile < counts[0]
        front_ok, front, front_here = entry(tile, 2)
        back_ok, back, back_here = entry(tile, 3)
        lower_ok, lower, _ = entry(tile, 4)
        upper_ok, upper, _ = entry(tile, 5)
        first = core == 0
        lower = jnp.where(first, lower, tile)
        lower_ok = jnp.where(first, lower_ok, filled)
        upper = jnp.where(first, tile, upper)
        upper_ok = jnp.where(first, filled, upper_ok)
        result = []
        for species in range(2):
            rate = diffusion[species]
            if step == 0:
                shift = 0
                from_front = jnp.where(front_here, y_here[species, front], y_minus[0][species, front])
                from_back = jnp.where(back_here, y_here[species, back], y_plus[0][species, back])
            else:
                shift = species
                from_front = jnp.where(front_here, y_high[step, front], y_minus[step][front])
                from_back = jnp.where(back_here, y_low[step, back], y_plus[step][back])
            from_front = jnp.where(front_ok, from_front, zero)
            from_back = jnp.where(back_ok, from_back, zero)
            ghost_y = rate * jnp.where(
                even, roll(from_front, 1 - EY - shift), roll(from_back, EY - 1 - shift)
            )
            below = rate * jnp.where(lower_ok, z_minus[step][species, lower], zero)
            above = rate * jnp.where(upper_ok, z_plus[step][species, upper], zero)
            values = []
            for j in range(columns):
                at = slice(j * LANES, (j + 1) * LANES)
                edge = jnp.concatenate(
                    [roll(ghost_y, -2 * (zv * columns + j)) for zv in range(half // ROWS)], axis=0
                )
                value = field[later, species, tile, :, at] + jnp.where(at_edge, edge, zero)
                value = value + jnp.where(row == 0, below[:, at], zero)
                value = value + jnp.where(row == half - 1, above[:, at], zero)
                values.append(value)
            result.append(values)
        return result

    def inner_step(step):
        def body(tile, carry):
            inner(step, tile)
            return carry

        lax.fori_loop(0, slots, body, 0)

    def outer_step(step):
        later = (step + 1) % 2

        def body(tile, carry):
            result = outer(step, tile)
            for species in range(2):
                for j in range(columns):
                    at = slice(j * LANES, (j + 1) * LANES)
                    field[later, species, tile, :, at] = result[species][j]
            put_faces(step + 1, tile, result)
            return carry

        lax.fori_loop(0, slots, body, 0, unroll=True)

    def give(tile):
        return pltpu.make_async_remote_copy(
            src_ref=stage.at[tile], dst_ref=out.at[0, tile, own_rows, :],
            send_sem=out_send.at[tile], recv_sem=out_recv.at[tile],
            device_id=partner_id, device_id_type=MESH,
        )

    def take(tile):
        return pltpu.make_async_remote_copy(
            src_ref=stage.at[tile], dst_ref=out.at[0, tile, other_rows, :],
            send_sem=out_send.at[tile], recv_sem=out_recv.at[tile],
            device_id=partner_id, device_id_type=MESH,
        )

    loads[0].wait()
    loads[1].wait()
    lax.fori_loop(0, slots, first_faces, 0, unroll=True)
    for wanted, copy in first_sends():
        pl.when(wanted)(copy.start)
    own_planes()
    loads[2].wait()
    swap_in.wait_recv()
    lax.fori_loop(0, slots, other_faces, 0, unroll=True)
    for step in range(STEPS):
        inner_step(step)
        if step == 0:
            wait_first()
        else:
            wait_faces(step)
        if step < STEPS - 1:
            outer_step(step)
            send_faces(step + 1)

    def last_body(tile, carry):
        result = outer(STEPS - 1, tile)
        for j in range(columns):
            at = slice(j * LANES, (j + 1) * LANES)
            stage[tile, :, at] = jnp.where(core == 0, result[1][j], result[0][j])
        give(tile).start()
        for j in range(columns):
            at = slice(j * LANES, (j + 1) * LANES)
            out[0, tile, own_rows, at] = jnp.where(core == 0, result[0][j], result[1][j])
        return carry

    lax.fori_loop(0, slots, last_body, 0, unroll=True)
    swap.wait_send()
    for wanted, copy in first_sends():
        pl.when(wanted)(copy.wait_send)
    for step in range(1, STEPS):
        wait_sent(step)
    for tile in range(slots):
        give(tile).wait_send()
        take(tile).wait_recv()


def per_device(layers, bands, ligand, density, counts, neighbours, diffusion, uptake):
    _, slots, depth, cells = ligand.shape
    half = depth // 2
    faces = (slots, ROWS, LANES)
    planes = (2, slots, 1, cells)
    smem = pl.BlockSpec(memory_space=pltpu.SMEM)
    away = pl.BlockSpec(memory_space=pltpu.HBM)
    return pl.pallas_call(
        functools.partial(kernel, layers, bands, slots, half, cells),
        out_shape=jax.ShapeDtypeStruct(ligand.shape, jnp.float32),
        in_specs=[smem, smem, smem, smem, away, away],
        out_specs=pl.BlockSpec(memory_space=pltpu.VMEM),
        scratch_shapes=[
            pltpu.VMEM((2, 2, slots, half, cells), jnp.float32),
            pltpu.VMEM((slots, half, cells), jnp.int32),
            pltpu.VMEM((slots, half, cells), jnp.float32),
            pltpu.VMEM((STEPS,) + faces, jnp.float32),
            pltpu.VMEM((STEPS,) + faces, jnp.float32),
            [pltpu.VMEM((2,) + faces, jnp.float32)] + [pltpu.VMEM(faces, jnp.float32)] * (STEPS - 1),
            [pltpu.VMEM((2,) + faces, jnp.float32)] + [pltpu.VMEM(faces, jnp.float32)] * (STEPS - 1),
            pltpu.VMEM((STEPS,) + planes, jnp.float32),
            pltpu.VMEM((STEPS,) + planes, jnp.float32),
            [pltpu.VMEM(planes, jnp.float32)] * STEPS,
            [pltpu.VMEM(planes, jnp.float32)] * STEPS,
            pltpu.VMEM((slots, half, cells), jnp.float32),
            pltpu.VMEM((2,) + faces, jnp.float32),
            pltpu.VMEM((2,) + faces, jnp.float32),
            pltpu.VMEM(planes, jnp.float32),
            pltpu.VMEM(planes, jnp.float32),
            pltpu.SemaphoreType.DMA((8,)),
            pltpu.SemaphoreType.DMA((4, 2)),
            pltpu.SemaphoreType.DMA((3,)),
            pltpu.SemaphoreType.DMA,
            pltpu.SemaphoreType.DMA,
            pltpu.SemaphoreType.DMA((STEPS, 4)),
            pltpu.SemaphoreType.DMA((STEPS, 4)),
            pltpu.SemaphoreType.DMA((slots,)),
            pltpu.SemaphoreType.DMA((slots,)),
        ],
        compiler_params=pltpu.CompilerParams(
            collective_id=0, has_side_effects=True, vmem_limit_bytes=53 * 1024 * 1024
        ),
    )(neighbours, counts, diffusion, uptake, ligand, density)


def solution(mesh):
    in_specs = (
        P("pair", ("groups", "cube", "row"), None, None),
        P(("groups", "cube", "row"), None, None),
        P(("groups", "cube", "row")),
        P(("groups", "cube", "row"), None),
        P(),
        P(),
    )
    out_specs = P("pair", ("groups", "cube", "row"), None, None)
    return jax.shard_map(
        functools.partial(per_device, mesh.shape["cube"], mesh.shape["row"]),
        mesh=mesh, in_specs=in_specs, out_specs=out_specs, check_vma=False,
    )
```
